32 devices in a mesh: wide: 16 (over z, y, x), narrow: 2 (over core).
Axes of the slice: x: 2, y: 2, z: 4, core: 2. Of those that a mesh axis runs over, the one named last changes fastest.
Arguments:
- tokens: bfloat16 [16384, 2048], P('wide', 'narrow'), may hold values from -6 to 6
- attn_gain: bfloat16 [2048], replicated, may hold values from 0.5 to 1.5
- q_weight: bfloat16 [2048, 3072], P('wide', 'narrow'), may hold values from -6 to 6
- kva_weight: bfloat16 [2048, 576], P('wide'), may hold values from -0.125 to 0.125
- kv_gain: bfloat16 [512], replicated, may hold values from 0.5 to 1.5
- kvb_weight: bfloat16 [512, 4096], P(None, 'narrow'), may hold values from -0.25 to 0.25
- o_weight: bfloat16 [2048, 2048], P('narrow'), may hold values from -0.125 to 0.125
- adapter_down: bfloat16 [2048, 1024], P(None, 'narrow'), may hold values from -0.125 to 0.125
- adapter_up_weight: bfloat16 [1024, 3072], P(None, 'narrow'), may hold values from -1.5 to 1.5
- lengths: int32 [16, 4], P('wide'), may hold values from 1 to 512, 1024 in all within a row
- adapter_ids: int32 [16, 4], P('wide'), may hold values from 0 to 63
- adapter_slot: int32 [64], replicated, may hold values from 0 to 63, each once
Outputs:
- hidden: bfloat16 [16384, 2048], P('wide', 'narrow')
- latent_cache: bfloat16 [16384, 576], P('wide')
The draws below stay inside these ranges and needn't reach their ends.
Inputs may be any that keep to these rules, and one draw needn't show every extreme that they name: Each row of lengths sums to 1024, and its longest prompt is exactly 512.
All inputs are finite; a program needn't handle non-finite values.
Results may differ from the reference program's by a relative error of at most 0.0095.
The reference program's roundings to bfloat16 on the way count: a program that leaves them out, or rounds other values in their place, can miss the bound.
Values may be sent and summed in bfloat16 or wider, within the bound.
A program may use at most 192 MiB of HBM per device.

```python
import math
import jax
import jax.numpy as jnp
import numpy as np
from jax import lax

D = 2048
HEADS = 16
NOPE = 128
ROPE = 64
VDIM = 128
LATENT = 512
RANK = 16
ADAPTERS = 64
PROMPT_DEV = 4
TOK_DEV = 1024
TOKENS = 16384
LMAX = 512
N_WIDE = 16
N_NARROW = 2


def draw_q_weight(key, part):
    base_key = jax.random.fold_in(key, 11)
    first_key = jax.random.fold_in(base_key, 0)
    values = jnp.clip(jax.random.normal(first_key, (D, HEADS, NOPE + ROPE), jnp.float32), -4.0, 4.0)
    values = values * float(D) ** (-0.5)
    return values.reshape(D, HEADS * (NOPE + ROPE)).astype(jnp.bfloat16)


def with_ends(entries, own_key, least, high):
    spot = [jax.random.randint(jax.random.fold_in(own_key, axis), (), 0, length) for axis, length in enumerate(entries.shape)]
    main_axis = entries.shape.index(max(entries.shape))
    next_to = spot[:main_axis] + [(spot[main_axis] + 1) % entries.shape[main_axis]] + spot[main_axis + 1:]
    return entries.at[tuple(spot)].set(least).at[tuple(next_to)].set(high)


def levels(key, shape, cuts, low, top_value):
    factor_of = 1.0
    for dim, parts in cuts:
        draws = jax.random.uniform(jax.random.fold_in(jax.random.fold_in(key, 6), dim), (parts,), jnp.float32, low / len(cuts), top_value / len(cuts))
        factor_of = factor_of * jnp.repeat(jnp.exp(draws), shape[dim] // parts).reshape((-1,) + (1,) * (len(shape) - 1 - dim))
    return factor_of


def profile(count, total, bound, slope):
    portions = [(1 << 20) // math.isqrt(standing ** slope) + 1 for standing in range(2, count + 1)]
    rest, holding = total - bound - (count - 1), [1] * (count - 1)
    while rest > 0:
        free = [i for i in range(count - 1) if holding[i] < bound]
        whole, remaining = sum([portions[i] for i in free]), rest
        for i in free:
            extra = min(bound - holding[i], max(1, remaining * portions[i] // whole), rest)
            holding[i] = holding[i] + extra
            rest = rest - extra
    return np.array([bound] + holding)


def ragged_sizes(own_key, amount, total, bound, skew):
    if amount == 2:
        one = jax.random.randint(own_key, (), max(1, total - bound), min(bound, total - 1) + 1)
        return jnp.stack([one, total - one])
    tallies = jnp.asarray(profile(amount, total, bound, skew), jnp.int32)
    pairs = (amount - 1) // 2
    giver, taker = tallies[1:1 + 2 * pairs:2], tallies[2:2 + 2 * pairs:2]
    slack = jnp.minimum(giver - 1, bound - taker)
    passed = jax.random.randint(jax.random.fold_in(own_key, 1), (pairs,), 0, 1 << 20) % (slack + 1)
    tallies = tallies.at[1:1 + 2 * pairs:2].set(giver - passed).at[2:2 + 2 * pairs:2].set(taker + passed)
    return tallies[jax.random.permutation(jax.random.fold_in(own_key, 2), amount)]


def normal_values(own_key, dims, deviation, bound, pieces=(), kind=jnp.bfloat16):
    result = deviation * jax.random.normal(own_key, dims, jnp.float32)
    if pieces:
        result = result * levels(own_key, dims, pieces, -0.22, 0.18)
    return jnp.clip(result, -bound, bound).astype(kind)


def setup_inputs(seed: int = 0) -> dict:
    seeds = jax.random.split(jax.random.key(seed), 13)
    tokens = normal_values(seeds[0], (TOKENS, D), 1.0, 6.0, ((0, 16), (1, 2)))
    attn_gain = jnp.clip(1.0 + 0.1 * jax.random.normal(seeds[1], (D,), jnp.float32), 0.5, 1.5).astype(jnp.bfloat16)
    q_weight = draw_q_weight(jax.random.fold_in(seeds[12], 71), 0)
    kva_weight = normal_values(seeds[3], (D, LATENT + ROPE), D ** -0.5, 0.125, ((0, 16),))
    kv_gain = jnp.clip(1.0 + 0.1 * jax.random.normal(seeds[4], (LATENT,), jnp.float32), 0.5, 1.5).astype(jnp.bfloat16)
    kvb_weight = normal_values(seeds[5], (LATENT, HEADS * (NOPE + VDIM)), LATENT ** -0.5, 0.25, ((1, 2),))
    o_weight = normal_values(seeds[6], (HEADS * VDIM, D), (HEADS * VDIM) ** -0.5, 0.125, ((0, 2),))
    adapter_down = normal_values(seeds[7], (D, ADAPTERS * RANK), D ** -0.5, 0.125, ((1, 2),))
    adapter_up_weight = normal_values(seeds[8], (ADAPTERS * RANK, HEADS * (NOPE + ROPE)), RANK ** -0.5, 1.5, ((1, 2),))
    lengths = jax.vmap(lambda own: ragged_sizes(own, PROMPT_DEV, TOK_DEV, LMAX, 2))(jax.random.split(seeds[9], N_WIDE)).reshape((N_WIDE, PROMPT_DEV)).astype(jnp.int32)
    adapter_ids = with_ends(jax.random.randint(seeds[10], (N_WIDE, PROMPT_DEV), 0, ADAPTERS), jax.random.fold_in(seeds[10], 1), 0, ADAPTERS - 1).astype(jnp.int32)
    adapter_slot = jax.random.permutation(seeds[11], ADAPTERS).astype(jnp.int32)
    return {"tokens": tokens, "attn_gain": attn_gain, "q_weight": q_weight, "kva_weight": kva_weight, "kv_gain": kv_gain, "kvb_weight": kvb_weight, "o_weight": o_weight, "adapter_down": adapter_down, "adapter_up_weight": adapter_up_weight, "lengths": lengths, "adapter_ids": adapter_ids, "adapter_slot": adapter_slot}


EPS = 1e-06
THETA = 50000.0
ADAPTER_SCALE = 2.0

def rms_scale(values, gain):
    mean_sq = lax.optimization_barrier(jnp.mean(values * values, axis=-1, keepdims=True))
    return values * lax.rsqrt(mean_sq + EPS) * gain.astype(jnp.float32)

def rotate(values, positions):
    half = values.shape[-1] // 2
    freqs = jnp.exp(-jnp.log(THETA) * 2.0 * jnp.arange(half).astype(jnp.float32) / (2 * half))
    angle = positions.astype(jnp.float32)[:, None] * freqs[None, :]
    cosine = jnp.cos(angle)
    sine = jnp.sin(angle)
    if values.ndim == 3:
        cosine = cosine[:, None, :]
        sine = sine[:, None, :]
    first = values[..., :half]
    second = values[..., half:]
    return jnp.concatenate([first * cosine - second * sine, first * sine + second * cosine], axis=-1)

def token_tables(length_row, id_row, adapter_slot, local_pos):
    ends = jnp.cumsum(length_row).astype(jnp.int32)
    starts = (ends - length_row).astype(jnp.int32)
    prompt = lax.optimization_barrier(jnp.sum((ends[None, :] <= local_pos[:, None]).astype(jnp.int32), axis=1)).astype(jnp.int32)
    onehot = (prompt[:, None] == jnp.arange(length_row.shape[0]).astype(jnp.int32)[None, :]).astype(jnp.int32)
    position = (local_pos - lax.optimization_barrier(jnp.sum(onehot * starts[None, :], axis=1))).astype(jnp.int32)
    adapter = lax.optimization_barrier(jnp.sum(onehot * id_row[None, :], axis=1)).astype(jnp.int32)
    slot_hot = (adapter[:, None] == jnp.arange(adapter_slot.shape[0]).astype(jnp.int32)[None, :]).astype(jnp.int32)
    slot = lax.optimization_barrier(jnp.sum(slot_hot * adapter_slot[None, :], axis=1)).astype(jnp.int32)
    return (prompt, position, adapter, slot)

def reference(tokens, attn_gain, q_weight, kva_weight, kv_gain, kvb_weight, o_weight, adapter_down, adapter_up_weight, lengths, adapter_ids, adapter_slot):
    total = tokens.shape[0]
    block = total // N_WIDE
    local_pos = jnp.arange(block).astype(jnp.int32)
    tables = jax.vmap(lambda lr, ir: token_tables(lr, ir, adapter_slot, local_pos))(lengths, adapter_ids)
    prompt, position, adapter, slot = [v.reshape(total).astype(jnp.int32) for v in tables]
    normed = rms_scale(tokens.astype(jnp.float32), attn_gain).astype(jnp.bfloat16)
    query_vectors = jnp.dot(normed, q_weight, preferred_element_type=jnp.float32)
    low = jnp.dot(normed, adapter_down, preferred_element_type=jnp.float32).reshape(total, ADAPTERS, RANK)
    pick = (slot[:, None] == jnp.arange(ADAPTERS).astype(jnp.int32)[None, :]).astype(jnp.float32)
    lowrank = lax.optimization_barrier(jnp.sum(low * pick[:, :, None], axis=1)).astype(jnp.bfloat16)
    usage = (adapter[:, None] == jnp.arange(ADAPTERS).astype(jnp.int32)[None, :]).astype(jnp.bfloat16)
    spread_rows = (usage[:, :, None] * lowrank[:, None, :]).reshape(total, ADAPTERS * RANK)
    query_vectors = query_vectors + ADAPTER_SCALE * jnp.dot(spread_rows, adapter_up_weight, preferred_element_type=jnp.float32)
    query_vectors = query_vectors.reshape(total, HEADS, NOPE + ROPE)
    query_vectors = jnp.concatenate([query_vectors[..., :NOPE], rotate(query_vectors[..., NOPE:], position)], axis=-1).astype(jnp.bfloat16)
    kv_pre = jnp.dot(normed, kva_weight, preferred_element_type=jnp.float32)
    latent = rms_scale(kv_pre[:, :LATENT], kv_gain).astype(jnp.bfloat16)
    key_rope = rotate(kv_pre[:, LATENT:], position).astype(jnp.bfloat16)
    latent_cache = jnp.concatenate([latent, key_rope], axis=1)
    expanded = jnp.dot(latent, kvb_weight, preferred_element_type=jnp.float32).astype(jnp.bfloat16)
    expanded = expanded.reshape(total, HEADS, NOPE + VDIM)
    scale = 1.0 / jnp.sqrt(jnp.float32(NOPE + ROPE))

    def attend(index):
        first = (index * block).astype(jnp.int32)
        query_block = lax.dynamic_slice_in_dim(query_vectors, first, block, 0).astype(jnp.float32)
        ex = lax.dynamic_slice_in_dim(expanded, first, block, 0).astype(jnp.float32)
        kr = lax.dynamic_slice_in_dim(key_rope, first, block, 0).astype(jnp.float32)
        pr = lax.dynamic_slice_in_dim(prompt, first, block, 0)
        scores = jnp.einsum('qhd,khd->hqk', query_block[..., :NOPE], ex[..., :NOPE])
        scores = (scores + jnp.einsum('qhd,kd->hqk', query_block[..., NOPE:], kr)) * scale
        allowed = (pr[None, :] == pr[:, None]) & (local_pos[None, :] <= local_pos[:, None])
        scores = jnp.where(allowed[None, :, :], scores, jnp.float32(-1e+30))
        top = lax.optimization_barrier(jnp.max(scores, axis=-1, keepdims=True))
        expo = jnp.exp(scores - top)
        weights = (expo / lax.optimization_barrier(jnp.sum(expo, axis=-1, keepdims=True))).astype(jnp.bfloat16)
        out = jnp.einsum('hqk,khd->qhd', weights.astype(jnp.float32), ex[..., NOPE:]).astype(jnp.bfloat16)
        return out.reshape(block, HEADS * VDIM)
    attended = lax.map(attend, jnp.arange(N_WIDE).astype(jnp.int32)).reshape(total, HEADS * VDIM)
    group = HEADS * VDIM // N_NARROW
    projected = jnp.zeros((total, D), jnp.float32)
    for index in range(N_NARROW):
        part = jnp.dot(attended[:, index * group:(index + 1) * group], o_weight[index * group:(index + 1) * group, :], preferred_element_type=jnp.float32)
        part = lax.optimization_barrier(part.astype(jnp.bfloat16))
        projected = projected + part.astype(jnp.float32)
    hidden = (tokens.astype(jnp.float32) + projected).astype(jnp.bfloat16)
    return (hidden, latent_cache)
```

```python
import functools
import math

import jax
import jax.numpy as jnp
from jax import lax
from jax.experimental import pallas as pl
from jax.experimental.pallas import tpu as pltpu
from jax.sharding import PartitionSpec as P

NOPE = 128
ROPE = 64
VDIM = 128
LATENT = 512
RANK = 16
LMAX = 512

EPS = 1e-06
THETA = 50000.0
ADAPTER_SCALE = 2.0

PAIR = 2 * (NOPE + ROPE)
TILE = 256
BAND = TILE + LMAX
MESH = pl.DeviceIdType.MESH
F32 = jnp.float32
BF16 = jnp.bfloat16


def axes_of(wide):
    side = math.isqrt(wide // 4)
    if wide % 4 == 0 and side * side * 4 == wide:
        return 4, side, side
    return wide, 1, 1


def iota(shape, dim):
    return lax.broadcasted_iota(jnp.int32, shape, dim)


def permute_pair(block):
    return jnp.concatenate(
        [
            block[:, :NOPE],
            block[:, NOPE + ROPE : 2 * NOPE + ROPE],
            block[:, NOPE : NOPE + ROPE],
            block[:, 2 * NOPE + ROPE :],
        ],
        axis=1,
    )


def turn(values, cosine, sine):
    low_half = (iota(values.shape, 1) & (ROPE - 1)) < ROPE // 2
    swapped = jnp.where(
        low_half,
        pltpu.roll(values, 2 * ROPE - ROPE // 2, 1),
        pltpu.roll(values, ROPE // 2, 1),
    )
    return values * cosine + swapped * sine


def kernel(
    dims,
    tokens,
    attn_gain,
    q_weight,
    kva_weight,
    kv_gain,
    kvb_weight,
    o_weight,
    adapter_down,
    adapter_up,
    lengths,
    ids,
    slots,
    hidden,
    cache,
    xbuf,
    normed,
    qstage,
    wq,
    wk,
    kvb,
    obuf,
    down,
    up,
    upsel,
    expanded,
    krot,
    latbuf,
    att,
    sendbuf,
    recvbuf,
    hbuf,
    bias,
    cosines,
    sines,
    low,
    low_other,
    spread,
    load_sem,
    store_sem,
    p1_send,
    p1_recv,
    p2_send,
    p2_recv,
    p3_send,
    p3_recv,
    core_send,
    core_recv,
    out_send,
    out_recv,
):
    nz, ny, nx = dims
    chunks = wq.shape[0]
    rows, half = tokens.shape
    tiles = rows // TILE
    depth = q_weight.shape[0]
    hd = depth // 2
    prompts = lengths.shape[1]
    wide = lax.axis_index("wide")
    core = lax.axis_index("narrow")
    x = wide % nx
    y = (wide // nx) % ny
    z = wide // (nx * ny)
    sib = 1 - core

    def at(zz, yy, xx):
        return (zz * ny + yy) * nx + xx

    def z_peer(d):
        return (at((z + d) % nz, y, x), core)

    def p_at(d):
        yy = (y + d * core) % ny
        xx = (x + d * (1 - core)) % nx
        return yy, xx

    def p_peer(d):
        yy, xx = p_at(d)
        return (at(z, yy, xx), core)

    def q_at(d):
        yy = (y + d * (1 - core)) % ny
        xx = (x + d * core) % nx
        return yy, xx

    def q_peer(d):
        yy, xx = q_at(d)
        return (at(z, yy, xx), core)

    def remote(src, dst, send, recv, device):
        return pltpu.make_async_remote_copy(
            src_ref=src, dst_ref=dst, send_sem=send, recv_sem=recv,
            device_id=device, device_id_type=MESH,
        )

    def piece(k, zz, yy, xx):
        if k == 0:
            return wk.at[zz, yy, xx, core]
        return wq.at[k - 1, zz, yy, xx]

    def p1(k, d):
        mine = piece(k, z, y, x)
        return remote(mine, mine, p1_send.at[k, d - 1], p1_recv.at[k, d - 1], z_peer(d))

    def p1_got(k, d):
        theirs = piece(k, (z - d + nz) % nz, y, x)
        return remote(theirs, theirs, p1_send.at[k, d - 1], p1_recv.at[k, d - 1], z_peer(d))

    def start_p1(k):
        for d in range(1, nz):
            p1(k, d).start()

    def wait_p1(k):
        for d in range(1, nz):
            p1_got(k, d).wait_recv()

    def column(k, yy, xx):
        return piece(k, slice(None), yy, xx)

    def start_p2(k):
        for d in range(1, nx):
            mine = column(k, y, x)
            remote(mine, mine, p2_send.at[k, d - 1], p2_recv.at[k, d - 1], p_peer(d)).start()

    def wait_p2(k):
        for d in range(1, nx):
            theirs = column(k, *p_at(nx - d))
            remote(theirs, theirs, p2_send.at[k, d - 1], p2_recv.at[k, d - 1], p_peer(d)).wait_recv()

    def plane(k, d, first):
        yy, xx = q_at(d)
        if first:
            return piece(k, slice(None), yy, slice(None))
        return piece(k, slice(None), slice(None), xx)

    def each_core(body):
        @pl.when(core == 0)
        def _():
            body(True)

        @pl.when(core == 1)
        def _():
            body(False)

    def start_p3(k):
        def body(first):
            for d in range(1, nx):
                mine = plane(k, 0, first)
                remote(mine, mine, p3_send.at[k, d - 1], p3_recv.at[k, d - 1], q_peer(d)).start()

        if nx > 1:
            each_core(body)

    def wait_p3(k):
        def body(first):
            for d in range(1, nx):
                theirs = plane(k, nx - d, first)
                remote(theirs, theirs, p3_send.at[k, d - 1], p3_recv.at[k, d - 1], q_peer(d)).wait_recv()

        if nx > 1:
            each_core(body)

    def drain(k):
        for d in range(1, nz):
            p1(k, d).wait_send()
        for d in range(1, nx):
            mine = column(k, y, x)
            remote(mine, mine, p2_send.at[k, d - 1], p2_recv.at[k, d - 1], p_peer(d)).wait_send()

        def body(first):
            for d in range(1, nx):
                mine = plane(k, 0, first)
                remote(mine, mine, p3_send.at[k, d - 1], p3_recv.at[k, d - 1], q_peer(d)).wait_send()

        if nx > 1:
            each_core(body)

    loads = [
        pltpu.make_async_copy(q_weight, qstage, load_sem.at[0]),
        pltpu.make_async_copy(
            kva_weight.at[pl.ds(pl.multiple_of(core * hd, hd), hd)],
            wk.at[z, y, x, core],
            load_sem.at[1],
        ),
        pltpu.make_async_copy(tokens, xbuf.at[core], load_sem.at[2]),
        pltpu.make_async_copy(adapter_down, down, load_sem.at[3]),
        pltpu.make_async_copy(kvb_weight, kvb, load_sem.at[4]),
        pltpu.make_async_copy(adapter_up, up, load_sem.at[5]),
        pltpu.make_async_copy(o_weight.at[:, pl.ds(0, half)], obuf.at[0], load_sem.at[6]),
        pltpu.make_async_copy(o_weight.at[:, pl.ds(half, half)], obuf.at[1], load_sem.at[7]),
    ]
    for load in loads:
        load.start()

    barrier = pltpu.get_barrier_semaphore()
    peers = [(wide, sib)]
    peers += [z_peer(d) for d in range(1, nz)]
    peers += [p_peer(d) for d in range(1, nx)]
    peers += [q_peer(d) for d in range(1, nx)]
    for peer in peers:
        pl.semaphore_signal(barrier, inc=1, device_id=peer, device_id_type=MESH)
    loads[0].wait()
    for j in range(chunks):
        wq[j, z, y, x] = permute_pair(qstage[:, j * PAIR : (j + 1) * PAIR])
    loads[1].wait()
    pl.semaphore_wait(barrier, len(peers))

    start_p1(0)
    loads[2].wait()
    sib_tokens = remote(xbuf.at[core], xbuf.at[core], core_send.at[0], core_recv.at[0], (wide, sib))
    sib_tokens.start()
    for k in range(1, chunks + 1):
        start_p1(k)

    ends = []
    total = jnp.int32(0)
    for j in range(prompts):
        total = total + lengths[0, j]
        ends.append(total)
    starts = [ends[j] - lengths[0, j] for j in range(prompts)]

    def prompt_of(index):
        found = jnp.zeros_like(index)
        for end in ends:
            found = found + (index >= end).astype(jnp.int32)
        return found

    def by_prompt(prompt, values):
        out = jnp.zeros_like(prompt)
        for j, value in enumerate(values):
            out = jnp.where(prompt == j, value, out)
        return out

    def tile(i):
        return pl.ds(pl.multiple_of(i * TILE, TILE), TILE)

    def band_start(i):
        return jnp.maximum(i - LMAX // TILE, 0) * TILE

    def tables(i, _):
        index = iota((TILE, 128), 0) + i * TILE
        position = index - by_prompt(prompt_of(index), starts)
        lane = iota((TILE, 128), 1)
        step = (lane & (ROPE // 2 - 1)).astype(F32)
        freqs = jnp.exp(-math.log(THETA) * 2.0 * step / ROPE)
        angle = position.astype(F32) * freqs
        cosines[tile(i)] = jnp.cos(angle)
        sine = jnp.sin(angle)
        sines[tile(i)] = jnp.where((lane & (ROPE - 1)) < ROPE // 2, -sine, sine)
        query = iota((TILE, BAND), 0) + i * TILE
        key = iota((1, BAND), 1) + band_start(i)
        same = prompt_of(iota((TILE, 1), 0) + i * TILE) == prompt_of(key)
        bias[i] = jnp.where(same & (key <= query), 0.0, -1e30).astype(F32)
        return 0

    lax.fori_loop(0, tiles, tables, 0)
    wait_p1(0)
    start_p2(0)

    sib_tokens.wait_recv()
    gain = attn_gain[...].astype(F32)

    def norm(i, _):
        left = xbuf[0, tile(i)].astype(F32)
        right = xbuf[1, tile(i)].astype(F32)
        total_sq = jnp.sum(left * left, -1, keepdims=True) + jnp.sum(right * right, -1, keepdims=True)
        factor = lax.rsqrt(total_sq / (2 * half) + EPS)
        normed[tile(i), :half] = (left * factor * gain[:, :half]).astype(BF16)
        normed[tile(i), half:] = (right * factor * gain[:, half:]).astype(BF16)
        return 0

    lax.fori_loop(0, tiles, norm, 0)
    wait_p2(0)
    start_p3(0)
    wait_p1(1)
    start_p2(1)

    loads[3].wait()
    owned = down.shape[1]

    def slot_of(j):
        found = jnp.int32(0)
        for n in range(slots.shape[0]):
            found = found + jnp.where(ids[0, j] == n, slots[n], 0)
        return found - core * (owned // RANK)

    slot_values = [slot_of(j) for j in range(prompts)]

    def lowrank(i, _):
        every = jnp.dot(normed[tile(i)], down[...], preferred_element_type=F32)
        index = iota((TILE, 1), 0) + i * TILE
        slot = by_prompt(prompt_of(index), slot_values)
        kept = jnp.where((iota((TILE, owned), 1) >> 4) == slot, every, 0.0).astype(BF16)
        fold = ((iota((owned, 128), 0) & (RANK - 1)) == (iota((owned, 128), 1) & (RANK - 1)))
        low[tile(i)] = jnp.dot(
            kept, fold.astype(F32).astype(BF16), preferred_element_type=F32
        ).astype(BF16)
        return 0

    lax.fori_loop(0, tiles, lowrank, 0)
    sib_low = remote(low, low_other, core_send.at[1], core_recv.at[1], (wide, sib))
    sib_low.start()

    wait_p3(0)
    own_kva = wk.at[:, :, :, core]
    sib_kva = remote(own_kva, own_kva, core_send.at[2], core_recv.at[2], (wide, sib))
    sib_kva.start()
    wait_p2(1)
    start_p3(1)
    wait_p1(2)
    start_p2(2)

    loads[5].wait()
    row = iota((128, up.shape[0]), 0)
    wanted = jnp.full_like(row, -1)
    for n in range(prompts):
        wanted = jnp.where((row >> 4) == n, ids[0, n] * RANK + (row & (RANK - 1)), wanted)
    picker = (iota(row.shape, 1) == wanted).astype(F32).astype(BF16)
    for j in range(chunks):
        picked = jnp.dot(picker, up[:, j * PAIR : (j + 1) * PAIR], preferred_element_type=F32)
        upsel[j] = permute_pair(picked.astype(BF16))
    sib_low.wait_recv()

    def place(i, _):
        both = low[tile(i)].astype(F32) + low_other[tile(i)].astype(F32)
        prompt = prompt_of(iota((TILE, 128), 0) + i * TILE)
        spread[tile(i)] = jnp.where((iota((TILE, 128), 1) >> 4) == prompt, both, 0.0).astype(BF16)
        return 0

    lax.fori_loop(0, tiles, place, 0)

    loads[4].wait()
    theirs = wk.at[:, :, :, sib]
    remote(theirs, theirs, core_send.at[2], core_recv.at[2], (wide, sib)).wait_recv()
    gain2 = kv_gain[...].astype(F32)

    def keys(i, _):
        pre = jnp.dot(
            normed[tile(i)], wk[...].reshape(nz * ny * nx * depth, LATENT + ROPE),
            preferred_element_type=F32,
        )
        body = pre[:, :LATENT]
        factor = lax.rsqrt(jnp.mean(body * body, -1, keepdims=True) + EPS)
        latent = (body * factor * gain2).astype(BF16)
        rope = pre[:, LATENT:]
        rope = turn(jnp.concatenate([rope, rope], axis=1), cosines[tile(i)], sines[tile(i)])
        rope = rope.astype(BF16)
        krot[tile(i)] = rope
        latbuf[tile(i), :LATENT] = latent
        latbuf[tile(i), LATENT:] = rope[:, :ROPE]
        wide_kv = jnp.dot(latent, kvb[...], preferred_element_type=F32).astype(BF16)
        for h in range(2 * chunks):
            expanded[h, tile(i)] = wide_kv[:, h * 256 : (h + 1) * 256]
        return 0

    lax.fori_loop(0, tiles, keys, 0)
    save_cache = pltpu.make_async_copy(latbuf, cache, store_sem.at[tiles])
    save_cache.start()

    scale = (1.0 / math.sqrt(NOPE + ROPE)) * math.log2(math.e)

    def attend(j):
        def step(i, _):
            query = jnp.dot(
                normed[tile(i)], wq[j].reshape(nz * ny * nx * depth, PAIR),
                preferred_element_type=F32,
            )
            query = query + ADAPTER_SCALE * jnp.dot(
                spread[tile(i)], upsel[j], preferred_element_type=F32
            )
            rope = turn(query[:, 2 * NOPE :], cosines[tile(i)], sines[tile(i)])
            lane = iota(rope.shape, 1)
            band = pl.ds(pl.multiple_of(band_start(i), TILE), BAND)
            key_rope = krot[band]
            for h in range(2):
                own = (lane >= h * ROPE) & (lane < (h + 1) * ROPE)
                full = jnp.concatenate(
                    [query[:, h * NOPE : (h + 1) * NOPE], jnp.where(own, rope, 0.0)], axis=1
                ).astype(BF16)
                pair = expanded[2 * j + h, band]
                key = jnp.concatenate([pair[:, :NOPE], key_rope], axis=1)
                scores = lax.dot_general(
                    full, key, (((1,), (1,)), ((), ())), preferred_element_type=F32
                )
                scores = scores * scale + bias[i]
                expo = jnp.exp2(scores - jnp.max(scores, -1, keepdims=True))
                weights = (expo * (1.0 / jnp.sum(expo, -1, keepdims=True))).astype(BF16)
                out = jnp.dot(weights, pair[:, NOPE:], preferred_element_type=F32)
                att[j, tile(i), h * VDIM : (h + 1) * VDIM] = out.astype(BF16)
            return 0

        lax.fori_loop(0, tiles, step, 0)

    for j in range(chunks):
        k = j + 1
        if k + 1 <= chunks:
            wait_p2(k + 1)
            start_p3(k + 1)
        if k + 2 <= chunks:
            wait_p1(k + 2)
            start_p2(k + 2)
        wait_p3(k)
        attend(j)

    loads[6].wait()
    loads[7].wait()

    def heads_of(i):
        return jnp.concatenate([att[j, tile(i)] for j in range(chunks)], axis=1)

    def give(i):
        return remote(sendbuf.at[i], recvbuf.at[i], out_send.at[i], out_recv.at[i], (wide, sib))

    def project_away(i, _):
        part = jnp.dot(heads_of(i), obuf[sib], preferred_element_type=F32)
        sendbuf[i] = part.astype(BF16)
        give(i).start()
        return 0

    lax.fori_loop(0, tiles, project_away, 0)

    def save(i):
        return pltpu.make_async_copy(hbuf.at[i], hidden.at[tile(i)], store_sem.at[i])

    def project_here(i, _):
        part = jnp.dot(heads_of(i), obuf[core], preferred_element_type=F32)
        part = part.astype(BF16).astype(F32)
        give(i).wait_recv()
        part = part + recvbuf[i].astype(F32)
        hbuf[i] = (xbuf[core, tile(i)].astype(F32) + part).astype(BF16)
        save(i).start()
        return 0

    lax.fori_loop(0, tiles, project_here, 0)

    for k in range(chunks + 1):
        drain(k)
    sib_tokens.wait_send()
    sib_low.wait_send()
    sib_kva.wait_send()
    save_cache.wait()
    for i in range(tiles):
        give(i).wait_send()
        save(i).wait()


def body(
    wide,
    tokens,
    attn_gain,
    q_weight,
    kva_weight,
    kv_gain,
    kvb_weight,
    o_weight,
    adapter_down,
    adapter_up_weight,
    lengths,
    adapter_ids,
    adapter_slot,
):
    dims = axes_of(wide)
    nz, ny, nx = dims
    rows, half = tokens.shape
    depth = q_weight.shape[0]
    chunks = q_weight.shape[1] // PAIR
    tiles = rows // TILE
    heads = o_weight.shape[0] // VDIM
    any_spec = pl.BlockSpec(memory_space=pl.ANY)
    vmem = pl.BlockSpec(memory_space=pltpu.VMEM)
    smem = pl.BlockSpec(memory_space=pltpu.SMEM)
    dma = pltpu.SemaphoreType.DMA
    V = pltpu.VMEM
    line = max(nx - 1, 1)
    return pl.pallas_call(
        functools.partial(kernel, dims),
        out_shape=(
            jax.ShapeDtypeStruct((rows, half), BF16),
            jax.ShapeDtypeStruct((rows, LATENT + ROPE), BF16),
        ),
        in_specs=[any_spec, vmem, any_spec, any_spec, vmem]
        + [any_spec] * 4
        + [smem] * 3,
        out_specs=(any_spec, any_spec),
        scratch_shapes=[
            V((2, rows, half), BF16),
            V((rows, 2 * half), BF16),
            V(q_weight.shape, BF16),
            V((chunks, nz, ny, nx, depth, PAIR), BF16),
            V((nz, ny, nx, 2, depth // 2, LATENT + ROPE), BF16),
            V(kvb_weight.shape, BF16),
            V((2, o_weight.shape[0], half), BF16),
            V(adapter_down.shape, BF16),
            V(adapter_up_weight.shape, BF16),
            V((chunks, 128, PAIR), BF16),
            V((heads, rows, NOPE + VDIM), BF16),
            V((rows, 2 * ROPE), BF16),
            V((rows, LATENT + ROPE), BF16),
            V((chunks, rows, 2 * VDIM), BF16),
            V((tiles, TILE, half), BF16),
            V((tiles, TILE, half), BF16),
            V((tiles, TILE, half), BF16),
            V((tiles, TILE, BAND), F32),
            V((rows, 2 * ROPE), F32),
            V((rows, 2 * ROPE), F32),
            V((rows, 128), BF16),
            V((rows, 128), BF16),
            V((rows, 128), BF16),
            dma((8,)),
            dma((tiles + 1,)),
            dma((chunks + 1, nz - 1)),
            dma((chunks + 1, nz - 1)),
            dma((chunks + 1, line)),
            dma((chunks + 1, line)),
            dma((chunks + 1, line)),
            dma((chunks + 1, line)),
            dma((3,)),
            dma((3,)),
            dma((tiles,)),
            dma((tiles,)),
        ],
        compiler_params=pltpu.CompilerParams(
            collective_id=0, has_side_effects=True, vmem_limit_bytes=62 * 1024 * 1024
        ),
        name="latent_block",
    )(
        tokens,
        attn_gain.reshape(1, -1),
        q_weight,
        kva_weight,
        kv_gain.reshape(1, -1),
        kvb_weight,
        o_weight,
        adapter_down,
        adapter_up_weight,
        lengths,
        adapter_ids,
        adapter_slot,
    )


def solution(mesh):
    return jax.shard_map(
        functools.partial(body, mesh.shape["wide"]),
        mesh=mesh,
        in_specs=(
            P("wide", "narrow"),
            P(),
            P("wide", "narrow"),
            P("wide", None),
            P(),
            P(None, "narrow"),
            P("narrow", None),
            P(None, "narrow"),
            P(None, "narrow"),
            P("wide", None),
            P("wide", None),
            P(),
        ),
        out_specs=(P("wide", "narrow"), P("wide", None)),
        check_vma=False,
    )
```

```python
import functools
import math

import jax
import jax.numpy as jnp
from jax import lax
from jax.experimental import pallas as pl
from jax.experimental.pallas import tpu as pltpu
from jax.sharding import PartitionSpec as P

NOPE = 128
ROPE = 64
VDIM = 128
LATENT = 512
RANK = 16
LMAX = 512

EPS = 1e-06
THETA = 50000.0
ADAPTER_SCALE = 2.0

PAIR = 2 * (NOPE + ROPE)
TILE = 256
BAND = TILE + LMAX
MESH = pl.DeviceIdType.MESH
F32 = jnp.float32
BF16 = jnp.bfloat16


def axes_of(wide):
    side = math.isqrt(wide // 4)
    if wide % 4 == 0 and side * side * 4 == wide:
        return 4, side, side
    return wide, 1, 1


def iota(shape, dim):
    return lax.broadcasted_iota(jnp.int32, shape, dim)


def permute_pair(block):
    return jnp.concatenate(
        [
            block[:, :NOPE],
            block[:, NOPE + ROPE : 2 * NOPE + ROPE],
            block[:, NOPE : NOPE + ROPE],
            block[:, 2 * NOPE + ROPE :],
        ],
        axis=1,
    )


def turn(values, cosine, sine):
    low_half = (iota(values.shape, 1) & (ROPE - 1)) < ROPE // 2
    swapped = jnp.where(
        low_half,
        pltpu.roll(values, 2 * ROPE - ROPE // 2, 1),
        pltpu.roll(values, ROPE // 2, 1),
    )
    return values * cosine + swapped * sine


def kernel(
    dims,
    tokens,
    attn_gain,
    q_weight,
    kva_weight,
    kv_gain,
    kvb_weight,
    o_weight,
    adapter_down,
    adapter_up,
    lengths,
    ids,
    slots,
    hidden,
    cache,
    xbuf,
    normed,
    qstage,
    wq,
    wk,
    kvb,
    obuf,
    down,
    up,
    upsel,
    expanded,
    krot,
    latbuf,
    att,
    sendbuf,
    recvbuf,
    hbuf,
    bias,
    cosines,
    sines,
    low,
    low_other,
    spread,
    load_sem,
    store_sem,
    p1_send,
    p1_recv,
    p2_send,
    p2_recv,
    p3_send,
    p3_recv,
    core_send,
    core_recv,
    out_send,
    out_recv,
):
    nz, ny, nx = dims
    chunks = wq.shape[0]
    rows, half = tokens.shape
    tiles = rows // TILE
    depth = q_weight.shape[0]
    hd = depth // 2
    prompts = lengths.shape[1]
    wide = lax.axis_index("wide")
    core = lax.axis_index("narrow")
    x = wide % nx
    y = (wide // nx) % ny
    z = wide // (nx * ny)
    sib = 1 - core

    def at(zz, yy, xx):
        return (zz * ny + yy) * nx + xx

    def z_peer(d):
        return (at((z + d) % nz, y, x), core)

    def p_at(d):
        yy = (y + d * core) % ny
        xx = (x + d * (1 - core)) % nx
        return yy, xx

    def p_peer(d):
        yy, xx = p_at(d)
        return (at(z, yy, xx), core)

    def q_at(d):
        yy = (y + d * (1 - core)) % ny
        xx = (x + d * core) % nx
        return yy, xx

    def q_peer(d):
        yy, xx = q_at(d)
        return (at(z, yy, xx), core)

    def remote(src, dst, send, recv, device):
        return pltpu.make_async_remote_copy(
            src_ref=src, dst_ref=dst, send_sem=send, recv_sem=recv,
            device_id=device, device_id_type=MESH,
        )

    def piece(k, zz, yy, xx):
        if k == 0:
            return wk.at[zz, yy, xx, core]
        return wq.at[k - 1, zz, yy, xx]

    def p1(k, d):
        mine = piece(k, z, y, x)
        return remote(mine, mine, p1_send.at[k, d - 1], p1_recv.at[k, d - 1], z_peer(d))

    def p1_got(k, d):
        theirs = piece(k, (z - d + nz) % nz, y, x)
        return remote(theirs, theirs, p1_send.at[k, d - 1], p1_recv.at[k, d - 1], z_peer(d))

    def start_p1(k):
        for d in range(1, nz):
            p1(k, d).start()

    def wait_p1(k):
        for d in range(1, nz):
            p1_got(k, d).wait_recv()

    def column(k, yy, xx):
        return piece(k, slice(None), yy, xx)

    def start_p2(k):
        for d in range(1, nx):
            mine = column(k, y, x)
            remote(mine, mine, p2_send.at[k, d - 1], p2_recv.at[k, d - 1], p_peer(d)).start()

    def wait_p2(k):
        for d in range(1, nx):
            theirs = column(k, *p_at(nx - d))
            remote(theirs, theirs, p2_send.at[k, d - 1], p2_recv.at[k, d - 1], p_peer(d)).wait_recv()

    def plane(k, d, first):
        yy, xx = q_at(d)
        if first:
            return piece(k, slice(None), yy, slice(None))
        return piece(k, slice(None), slice(None), xx)

    def each_core(body):
        @pl.when(core == 0)
        def _():
            body(True)

        @pl.when(core == 1)
        def _():
            body(False)

    def start_p3(k):
        def body(first):
            for d in range(1, nx):
                mine = plane(k, 0, first)
                remote(mine, mine, p3_send.at[k, d - 1], p3_recv.at[k, d - 1], q_peer(d)).start()

        if nx > 1:
            each_core(body)

    def wait_p3(k):
        def body(first):
            for d in range(1, nx):
                theirs = plane(k, nx - d, first)
                remote(theirs, theirs, p3_send.at[k, d - 1], p3_recv.at[k, d - 1], q_peer(d)).wait_recv()

        if nx > 1:
            each_core(body)

    def drain(k):
        for d in range(1, nz):
            p1(k, d).wait_send()
        for d in range(1, nx):
            mine = column(k, y, x)
            remote(mine, mine, p2_send.at[k, d - 1], p2_recv.at[k, d - 1], p_peer(d)).wait_send()

        def body(first):
            for d in range(1, nx):
                mine = plane(k, 0, first)
                remote(mine, mine, p3_send.at[k, d - 1], p3_recv.at[k, d - 1], q_peer(d)).wait_send()

        if nx > 1:
            each_core(body)

    loads = [
        pltpu.make_async_copy(q_weight, qstage, load_sem.at[0]),
        pltpu.make_async_copy(
            kva_weight.at[pl.ds(pl.multiple_of(core * hd, hd), hd)],
            wk.at[z, y, x, core],
            load_sem.at[1],
        ),
        pltpu.make_async_copy(tokens, xbuf.at[core], load_sem.at[2]),
        pltpu.make_async_copy(adapter_down, down, load_sem.at[3]),
        pltpu.make_async_copy(kvb_weight, kvb, load_sem.at[4]),
        pltpu.make_async_copy(adapter_up, up, load_sem.at[5]),
        pltpu.make_async_copy(o_weight.at[:, pl.ds(0, half)], obuf.at[0], load_sem.at[6]),
        pltpu.make_async_copy(o_weight.at[:, pl.ds(half, half)], obuf.at[1], load_sem.at[7]),
    ]
    for load in loads:
        load.start()

    barrier = pltpu.get_barrier_semaphore()
    peers = [(wide, sib)]
    peers += [z_peer(d) for d in range(1, nz)]
    peers += [p_peer(d) for d in range(1, nx)]
    peers += [q_peer(d) for d in range(1, nx)]
    for peer in peers:
        pl.semaphore_signal(barrier, inc=1, device_id=peer, device_id_type=MESH)
    loads[0].wait()
    for j in range(chunks):
        wq[j, z, y, x] = permute_pair(qstage[:, j * PAIR : (j + 1) * PAIR])
    loads[1].wait()
    pl.semaphore_wait(barrier, len(peers))

    start_p1(0)
    loads[2].wait()
    sib_tokens = remote(xbuf.at[core], xbuf.at[core], core_send.at[0], core_recv.at[0], (wide, sib))
    sib_tokens.start()

    ends = []
    total = jnp.int32(0)
    for j in range(prompts):
        total = total + lengths[0, j]
        ends.append(total)
    starts = [ends[j] - lengths[0, j] for j in range(prompts)]

    def prompt_of(index):
        found = jnp.zeros_like(index)
        for end in ends:
            found = found + (index >= end).astype(jnp.int32)
        return found

    def by_prompt(prompt, values):
        out = jnp.zeros_like(prompt)
        for j, value in enumerate(values):
            out = jnp.where(prompt == j, value, out)
        return out

    def tile(i):
        return pl.ds(pl.multiple_of(i * TILE, TILE), TILE)

    def band_start(i):
        return jnp.maximum(i - LMAX // TILE, 0) * TILE

    def tables(i, _):
        index = iota((TILE, 128), 0) + i * TILE
        position = index - by_prompt(prompt_of(index), starts)
        lane = iota((TILE, 128), 1)
        step = (lane & (ROPE // 2 - 1)).astype(F32)
        freqs = jnp.exp(-math.log(THETA) * 2.0 * step / ROPE)
        angle = position.astype(F32) * freqs
        cosines[tile(i)] = jnp.cos(angle)
        sine = jnp.sin(angle)
        sines[tile(i)] = jnp.where((lane & (ROPE - 1)) < ROPE // 2, -sine, sine)
        query = iota((TILE, BAND), 0) + i * TILE
        key = iota((1, BAND), 1) + band_start(i)
        same = prompt_of(iota((TILE, 1), 0) + i * TILE) == prompt_of(key)
        bias[i] = jnp.where(same & (key <= query), 0.0, -1e30).astype(F32)
        return 0

    wait_p1(0)
    start_p2(0)
    start_p1(1)
    lax.fori_loop(0, tiles, tables, 0)

    wait_p2(0)
    start_p3(0)
    wait_p1(1)
    start_p2(1)
    start_p1(2)
    sib_tokens.wait_recv()
    gain = attn_gain[...].astype(F32).reshape(1, 2 * half)

    def norm(i, _):
        left = xbuf[0, tile(i)].astype(F32)
        right = xbuf[1, tile(i)].astype(F32)
        total_sq = jnp.sum(left * left, -1, keepdims=True) + jnp.sum(right * right, -1, keepdims=True)
        factor = lax.rsqrt(total_sq / (2 * half) + EPS)
        normed[tile(i), :half] = (left * factor * gain[:, :half]).astype(BF16)
        normed[tile(i), half:] = (right * factor * gain[:, half:]).astype(BF16)
        return 0

    lax.fori_loop(0, tiles, norm, 0)

    loads[3].wait()
    owned = down.shape[1]

    def slot_of(j):
        found = jnp.int32(0)
        for n in range(slots.shape[0]):
            found = found + jnp.where(ids[0, j] == n, slots[n], 0)
        return found - core * (owned // RANK)

    slot_values = [slot_of(j) for j in range(prompts)]

    def lowrank(i, _):
        every = jnp.dot(normed[tile(i)], down[...], preferred_element_type=F32)
        index = iota((TILE, 1), 0) + i * TILE
        slot = by_prompt(prompt_of(index), slot_values)
        kept = jnp.where((iota((TILE, owned), 1) >> 4) == slot, every, 0.0).astype(BF16)
        fold = ((iota((owned, 128), 0) & (RANK - 1)) == (iota((owned, 128), 1) & (RANK - 1)))
        low[tile(i)] = jnp.dot(
            kept, fold.astype(F32).astype(BF16), preferred_element_type=F32
        ).astype(BF16)
        return 0

    lax.fori_loop(0, tiles, lowrank, 0)
    sib_low = remote(low, low_other, core_send.at[1], core_recv.at[1], (wide, sib))
    sib_low.start()

    wait_p3(0)
    own_kva = wk.at[:, :, :, core]
    sib_kva = remote(own_kva, own_kva, core_send.at[2], core_recv.at[2], (wide, sib))
    sib_kva.start()
    wait_p2(1)
    start_p3(1)
    wait_p1(2)
    start_p2(2)
    start_p1(3)

    loads[5].wait()
    row = iota((128, up.shape[0]), 0)
    wanted = jnp.full_like(row, -1)
    for n in range(prompts):
        wanted = jnp.where((row >> 4) == n, ids[0, n] * RANK + (row & (RANK - 1)), wanted)
    picker = (iota(row.shape, 1) == wanted).astype(F32).astype(BF16)
    for j in range(chunks):
        picked = jnp.dot(picker, up[:, j * PAIR : (j + 1) * PAIR], preferred_element_type=F32)
        upsel[j] = permute_pair(picked.astype(BF16))
    sib_low.wait_recv()

    def place(i, _):
        both = low[tile(i)].astype(F32) + low_other[tile(i)].astype(F32)
        prompt = prompt_of(iota((TILE, 128), 0) + i * TILE)
        spread[tile(i)] = jnp.where((iota((TILE, 128), 1) >> 4) == prompt, both, 0.0).astype(BF16)
        return 0

    lax.fori_loop(0, tiles, place, 0)

    loads[4].wait()
    theirs = wk.at[:, :, :, sib]
    remote(theirs, theirs, core_send.at[2], core_recv.at[2], (wide, sib)).wait_recv()
    gain2 = kv_gain[...].astype(F32).reshape(1, LATENT)

    def keys(i, _):
        pre = jnp.dot(
            normed[tile(i)], wk[...].reshape(nz * ny * nx * depth, LATENT + ROPE),
            preferred_element_type=F32,
        )
        body = pre[:, :LATENT]
        factor = lax.rsqrt(jnp.mean(body * body, -1, keepdims=True) + EPS)
        latent = (body * factor * gain2).astype(BF16)
        rope = pre[:, LATENT:]
        rope = turn(jnp.concatenate([rope, rope], axis=1), cosines[tile(i)], sines[tile(i)])
        rope = rope.astype(BF16)
        krot[tile(i)] = rope
        latbuf[tile(i), :LATENT] = latent
        latbuf[tile(i), LATENT:] = rope[:, :ROPE]
        wide_kv = jnp.dot(latent, kvb[...], preferred_element_type=F32).astype(BF16)
        for h in range(2 * chunks):
            expanded[h, tile(i)] = wide_kv[:, h * 256 : (h + 1) * 256]
        return 0

    lax.fori_loop(0, tiles, keys, 0)
    save_cache = pltpu.make_async_copy(latbuf, cache, store_sem.at[tiles])
    save_cache.start()

    scale = (1.0 / math.sqrt(NOPE + ROPE)) * math.log2(math.e)

    def attend(j):
        def step(i, _):
            query = jnp.dot(
                normed[tile(i)], wq[j].reshape(nz * ny * nx * depth, PAIR),
                preferred_element_type=F32,
            )
            query = query + ADAPTER_SCALE * jnp.dot(
                spread[tile(i)], upsel[j], preferred_element_type=F32
            )
            rope = turn(query[:, 2 * NOPE :], cosines[tile(i)], sines[tile(i)])
            lane = iota(rope.shape, 1)
            band = pl.ds(pl.multiple_of(band_start(i), TILE), BAND)
            key_rope = krot[band]
            for h in range(2):
                own = (lane >= h * ROPE) & (lane < (h + 1) * ROPE)
                full = jnp.concatenate(
                    [query[:, h * NOPE : (h + 1) * NOPE], jnp.where(own, rope, 0.0)], axis=1
                ).astype(BF16)
                pair = expanded[2 * j + h, band]
                key = jnp.concatenate([pair[:, :NOPE], key_rope], axis=1)
                scores = lax.dot_general(
                    full, key, (((1,), (1,)), ((), ())), preferred_element_type=F32
                )
                scores = scores * scale + bias[i]
                expo = jnp.exp2(scores - jnp.max(scores, -1, keepdims=True))
                weights = (expo * (1.0 / jnp.sum(expo, -1, keepdims=True))).astype(BF16)
                out = jnp.dot(weights, pair[:, NOPE:], preferred_element_type=F32)
                att[j, tile(i), h * VDIM : (h + 1) * VDIM] = out.astype(BF16)
            return 0

        lax.fori_loop(0, tiles, step, 0)

    for j in range(chunks):
        k = j + 1
        if k + 1 <= chunks:
            wait_p2(k + 1)
            start_p3(k + 1)
        if k + 2 <= chunks:
            wait_p1(k + 2)
            start_p2(k + 2)
        if k + 3 <= chunks:
            start_p1(k + 3)
        wait_p3(k)
        attend(j)

    loads[6].wait()
    loads[7].wait()

    def heads_of(i):
        return jnp.concatenate([att[j, tile(i)] for j in range(chunks)], axis=1)

    def give(i):
        return remote(sendbuf.at[i], recvbuf.at[i], out_send.at[i], out_recv.at[i], (wide, sib))

    def project_away(i, _):
        part = jnp.dot(heads_of(i), obuf[sib], preferred_element_type=F32)
        sendbuf[i] = part.astype(BF16)
        give(i).start()
        return 0

    lax.fori_loop(0, tiles, project_away, 0)

    def save(i):
        return pltpu.make_async_copy(hbuf.at[i], hidden.at[tile(i)], store_sem.at[i])

    def project_here(i, _):
        part = jnp.dot(heads_of(i), obuf[core], preferred_element_type=F32)
        part = part.astype(BF16).astype(F32)
        give(i).wait_recv()
        part = part + recvbuf[i].astype(F32)
        hbuf[i] = (xbuf[core, tile(i)].astype(F32) + part).astype(BF16)
        save(i).start()
        return 0

    lax.fori_loop(0, tiles, project_here, 0)

    for k in range(chunks + 1):
        drain(k)
    sib_tokens.wait_send()
    sib_low.wait_send()
    sib_kva.wait_send()
    save_cache.wait()
    for i in range(tiles):
        give(i).wait_send()
        save(i).wait()


def body(
    wide,
    tokens,
    attn_gain,
    q_weight,
    kva_weight,
    kv_gain,
    kvb_weight,
    o_weight,
    adapter_down,
    adapter_up_weight,
    lengths,
    adapter_ids,
    adapter_slot,
):
    dims = axes_of(wide)
    nz, ny, nx = dims
    rows, half = tokens.shape
    depth = q_weight.shape[0]
    chunks = q_weight.shape[1] // PAIR
    tiles = rows // TILE
    heads = o_weight.shape[0] // VDIM
    any_spec = pl.BlockSpec(memory_space=pl.ANY)
    vmem = pl.BlockSpec(memory_space=pltpu.VMEM)
    smem = pl.BlockSpec(memory_space=pltpu.SMEM)
    dma = pltpu.SemaphoreType.DMA
    V = pltpu.VMEM
    line = max(nx - 1, 1)
    return pl.pallas_call(
        functools.partial(kernel, dims),
        out_shape=(
            jax.ShapeDtypeStruct((rows, half), BF16),
            jax.ShapeDtypeStruct((rows, LATENT + ROPE), BF16),
        ),
        in_specs=[any_spec, vmem, any_spec, any_spec, vmem]
        + [any_spec] * 4
        + [smem] * 3,
        out_specs=(any_spec, any_spec),
        scratch_shapes=[
            V((2, rows, half), BF16),
            V((rows, 2 * half), BF16),
            V(q_weight.shape, BF16),
            V((chunks, nz, ny, nx, depth, PAIR), BF16),
            V((nz, ny, nx, 2, depth // 2, LATENT + ROPE), BF16),
            V(kvb_weight.shape, BF16),
            V((2, o_weight.shape[0], half), BF16),
            V(adapter_down.shape, BF16),
            V(adapter_up_weight.shape, BF16),
            V((chunks, 128, PAIR), BF16),
            V((heads, rows, NOPE + VDIM), BF16),
            V((rows, 2 * ROPE), BF16),
            V((rows, LATENT + ROPE), BF16),
            V((chunks, rows, 2 * VDIM), BF16),
            V((tiles, TILE, half), BF16),
            V((tiles, TILE, half), BF16),
            V((tiles, TILE, half), BF16),
            V((tiles, TILE, BAND), F32),
            V((rows, 2 * ROPE), F32),
            V((rows, 2 * ROPE), F32),
            V((rows, 128), BF16),
            V((rows, 128), BF16),
            V((rows, 128), BF16),
            dma((8,)),
            dma((tiles + 1,)),
            dma((chunks + 1, nz - 1)),
            dma((chunks + 1, nz - 1)),
            dma((chunks + 1, line)),
            dma((chunks + 1, line)),
            dma((chunks + 1, line)),
            dma((chunks + 1, line)),
            dma((3,)),
            dma((3,)),
            dma((tiles,)),
            dma((tiles,)),
        ],
        compiler_params=pltpu.CompilerParams(
            collective_id=0, has_side_effects=True, vmem_limit_bytes=62 * 1024 * 1024
        ),
        name="latent_block",
    )(
        tokens,
        attn_gain,
        q_weight,
        kva_weight,
        kv_gain,
        kvb_weight,
        o_weight,
        adapter_down,
        adapter_up_weight,
        lengths,
        adapter_ids,
        adapter_slot,
    )


def solution(mesh):
    return jax.shard_map(
        functools.partial(body, mesh.shape["wide"]),
        mesh=mesh,
        in_specs=(
            P("wide", "narrow"),
            P(),
            P("wide", "narrow"),
            P("wide", None),
            P(),
            P(None, "narrow"),
            P("narrow", None),
            P(None, "narrow"),
            P(None, "narrow"),
            P("wide", None),
            P("wide", None),
            P(),
        ),
        out_specs=(P("wide", "narrow"), P("wide", None)),
        check_vma=False,
    )
```
